256 devices in a mesh: pipe: 8 (over x_lo, y), expert: 16 (over z, x_hi), dp: 2 (over core).
Axes of the slice: x: 4 (x_hi: 2, x_lo: 2; x = x_hi * 2 + x_lo), y: 4, z: 8, core: 2. Of those that a mesh axis runs over, the one named last changes fastest.
Arguments:
- states: bfloat16 [16, 1024, 3584], P(('pipe', 'dp'), 'expert'), may hold values from -6 to 6
- norm_gain: float32 [16, 3584], P(('pipe', 'dp')), may hold values from 0.4 to 1.6
- w_in: bfloat16 [16, 16, 3584, 1024], P(('pipe', 'dp'), 'expert'), may hold values from -0.09375 to 0.09375
- w_out: bfloat16 [16, 16, 512, 3584], P(('pipe', 'dp'), 'expert'), may hold values from -0.1875 to 0.1875
- routes: int32 [16, 2, 1024, 2], P(('pipe', 'dp'), None, 'expert'), may hold values from 0 to 7, all different within a row; in each aligned block of 64 rows (0 to 63, 64 to 127, ..., all dimensions but the last counted through in order) at most 20 rows name the same one
- route_weights: float32 [16, 2, 1024, 2], P(('pipe', 'dp'), None, 'expert'), may hold values from 0.2 to 1
Outputs:
- section_outputs: bfloat16 [16, 1024, 3584], P(('pipe', 'dp'), 'expert')
The draws below stay inside these ranges and needn't reach their ends.
Inputs may be any that keep to these rules, and one draw needn't show every extreme that they name: `routes`: each row names 2 different experts. In each aligned block of 64 rows (the tokens of one index of expert at one section and step) no expert is named by more than 20 rows.
All inputs are finite; a program needn't handle non-finite values.
Results may differ from the reference program's by a relative error of at most 0.0075.
Values may be sent and summed in bfloat16 or wider, within the bound.
A program may use at most 64 MiB of HBM per device.

```python
import math
import jax
import jax.numpy as jnp
import numpy as np
from jax import lax

D = 3584
FF = 1024
TOP = 2
STEPS = 2
TOK = 64
HOLDERS = 16
EXPERTS = 8
TOKENS = 1024
CAP = 20
N_PIPE = 8
N_EXPERT = 16


def level_of(stream_key, extent, split, smallest, high):
    loudness = 1.0
    for position, blocks in split:
        steps = jax.random.uniform(jax.random.fold_in(jax.random.fold_in(stream_key, 6), position), (blocks,), jnp.float32, smallest / len(split), high / len(split))
        loudness = loudness * jnp.repeat(jnp.exp(steps), extent[position] // blocks).reshape((-1,) + (1,) * (len(extent) - 1 - position))
    return loudness


def routed_block(stream_key, own, number, rows, amount, top, reach, slope):
    sequence = jax.random.permutation(stream_key, amount)
    packed, common = shares(amount, rows * top, reach, slope, True), shares(amount, rows * top, reach, slope, False)
    places = jnp.arange(amount)

    def named(lengths, offset_by):
        used = int((lengths > 0).sum())
        fixed = max(1, used // 4)
        shifted = fixed + (places - fixed + offset_by * (used - fixed)) % max(1, amount - fixed)
        return jnp.zeros((amount,), jnp.int32).at[sequence[jnp.where(places < fixed, places, shifted)]].set(jnp.asarray(lengths, jnp.int32))

    lengths = jnp.where(number % 4 == 0, named(packed, number // 4), named(common, number - number // 4 - 1))
    mixed = jax.random.permutation(jax.random.fold_in(own, 3), amount)
    donor, taker = mixed[0:amount // 2 * 2:2], mixed[1:amount // 2 * 2:2]
    room = jnp.minimum(lengths[donor] - 1, reach - lengths[taker]) // 2
    room = jnp.where((donor == sequence[0]) | (taker == sequence[0]) | (lengths[taker] == 0), 0, jnp.maximum(room, 0))
    shifted = jax.random.randint(jax.random.fold_in(own, 4), (amount // 2,), 0, 1 << 20) % (room + 1)
    lengths = lengths.at[donor].add(-shifted).at[taker].add(shifted)
    items = jnp.searchsorted(jnp.cumsum(lengths), jnp.arange(rows * top), side="right").astype(jnp.int32)
    listing = items.reshape(top, rows).T
    listing = listing[jax.random.permutation(jax.random.fold_in(own, 1), rows)]
    offset_by = jax.random.randint(jax.random.fold_in(own, 2), (rows, 1), 0, top)
    return jnp.take_along_axis(listing, (jnp.arange(top)[None, :] + offset_by) % top, axis=1)


def shares(number_of, total, bound, lean, full):
    loads = [(1 << 20) // math.isqrt(standing ** lean) + 1 for standing in range(1, number_of + 1)]
    largest = bound if full else min(bound, max(-(-total // number_of), total * loads[0] // sum(loads)))
    least = 1 if total - largest >= number_of - 1 else 0
    counts, rest = [largest] + [least] * (number_of - 1), total - largest - least * (number_of - 1)
    while rest > 0:
        free = [i for i in range(1, number_of) if counts[i] < largest] or [i for i in range(1, number_of) if counts[i] < bound]
        whole, remaining = sum([loads[i] for i in free]), rest
        for i in free:
            extra = min(bound - counts[i], max(1, remaining * loads[i] // whole), rest)
            counts[i] = counts[i] + extra
            rest = rest - extra
    return np.array(counts)


def gaussian(own_key, shape, deviation, most, split=(), kind=jnp.bfloat16):
    factor_of = level_of(own_key, shape, split, -0.22, 0.18) if split else 1.0
    entries = jax.random.normal(own_key, shape, jnp.float32) * deviation * factor_of
    return jnp.minimum(jnp.maximum(entries, -most), most).astype(kind)


def setup_inputs(seed: int = 0) -> dict:
    streams_of = jax.random.split(jax.random.key(seed), 7)
    states = gaussian(streams_of[0], (HOLDERS, TOKENS, D), 1.0, 6.0, ((0, 16), (1, 16)))
    norm_gain = jnp.clip(1.0 + 0.12 * jax.random.normal(streams_of[1], (HOLDERS, D), jnp.float32), 0.4, 1.6)
    w_in = gaussian(streams_of[2], (HOLDERS, 2 * EXPERTS, D, FF), D ** -0.5, 0.09375, ((0, 16), (1, 16)))
    w_out = gaussian(streams_of[3], (HOLDERS, 2 * EXPERTS, FF // 2, D), FF ** -0.5, 0.1875, ((0, 16), (1, 16)))
    routes_keys = jax.random.split(jax.random.fold_in(streams_of[4], 1), HOLDERS * STEPS * TOKENS // TOK)
    routes_turns = jax.random.permutation(jax.random.fold_in(streams_of[4], 3), HOLDERS * STEPS * TOKENS // TOK)
    routes = jax.vmap(lambda own, number: routed_block(jax.random.fold_in(streams_of[4], 2), own, number, TOK, EXPERTS, TOP, CAP, 2))(routes_keys, routes_turns).reshape((HOLDERS, STEPS, TOKENS, TOP))
    route_weights = jnp.clip(0.2 + 0.8 * jax.random.uniform(streams_of[5], (HOLDERS, STEPS, TOKENS, TOP), jnp.float32) ** level_of(streams_of[5], (HOLDERS, STEPS, TOKENS, TOP), ((0, 16), (2, 16)), -0.2, 0.2), 0.2, 1.0)
    return {"states": states, "norm_gain": norm_gain, "w_in": w_in, "w_out": w_out, "routes": routes, "route_weights": route_weights}


EPS = 1e-06

def chain_tables():
    holders = 2 * N_PIPE
    section_of = np.zeros(holders, np.int32)
    for holder in range(holders):
        pipe_rank = holder // 2
        section_of[holder] = pipe_rank if holder % 2 == 0 else holders - 1 - pipe_rank
    holder_of = np.zeros(holders, np.int32)
    for holder in range(holders):
        holder_of[section_of[holder]] = holder
    source = np.zeros(holders, np.int32)
    live = np.zeros(holders, np.float32)
    for holder in range(holders):
        if section_of[holder] > 0:
            source[holder] = holder_of[section_of[holder] - 1]
            live[holder] = 1.0
    return (source, live)

def slot_index(route_block):
    onehot = (route_block[:, :, None] == jnp.arange(EXPERTS, dtype=jnp.int32)).astype(jnp.int32)
    per_token = lax.optimization_barrier(jnp.sum(onehot, axis=1))
    earlier = jnp.cumsum(per_token, axis=0) - per_token
    return lax.optimization_barrier(jnp.sum(onehot * earlier[:, None, :], axis=2)).astype(jnp.int32)

def apply_section(current, gain, weight_in, weight_out, route_rows, weight_rows):
    blocks = current.reshape(N_EXPERT, TOK, D).astype(jnp.float32)
    normed = (blocks * lax.rsqrt(lax.optimization_barrier(jnp.mean(blocks * blocks, axis=-1, keepdims=True)) + EPS) * gain).astype(jnp.bfloat16)
    route_blocks = route_rows.reshape(N_EXPERT, TOK, TOP)
    slots = jax.vmap(slot_index)(route_blocks)
    flat = (route_blocks * CAP + slots).astype(jnp.int32)

    def fill(normed_block, flat_block):
        copies = jnp.broadcast_to(normed_block[:, None, :], (TOK, TOP, D)).reshape(TOK * TOP, D)
        return jnp.zeros((EXPERTS * CAP, D), jnp.bfloat16).at[flat_block.reshape(-1)].set(copies)
    buffers = jax.vmap(fill)(normed, flat).reshape(N_EXPERT, EXPERTS, CAP, D)

    def one_expert(operands):
        expert_rows, in_pair, out_pair = operands
        flat_rows = expert_rows.reshape(N_EXPERT * CAP, D)
        total = jnp.zeros((N_EXPERT * CAP, D), jnp.float32)
        for half_index in range(2):
            both = jnp.dot(flat_rows, in_pair[half_index], preferred_element_type=jnp.float32)
            hidden = (jax.nn.silu(both[:, :FF // 2]) * both[:, FF // 2:]).astype(jnp.bfloat16)
            partial_value = jnp.dot(hidden, out_pair[half_index], preferred_element_type=jnp.float32).astype(jnp.bfloat16)
            total = total + partial_value.astype(jnp.float32)
        return total.astype(jnp.bfloat16).reshape(N_EXPERT, CAP, D)
    results = lax.map(one_expert, (jnp.swapaxes(buffers, 0, 1), weight_in.reshape(EXPERTS, 2, D, FF), weight_out.reshape(EXPERTS, 2, FF // 2, D)))
    by_source = jnp.swapaxes(results, 0, 1).reshape(N_EXPERT, EXPERTS * CAP, D)
    picked = jax.vmap(lambda table, index: jnp.take(table, index, axis=0))(by_source, flat)
    mixed = blocks + lax.optimization_barrier(jnp.sum(weight_rows.reshape(N_EXPERT, TOK, TOP, 1) * picked.astype(jnp.float32), axis=2))
    return mixed.astype(jnp.bfloat16).reshape(TOKENS, D)

def reference(states, norm_gain, w_in, w_out, routes, route_weights):
    source, live = chain_tables()
    live_mask = jnp.asarray(live)[:, None, None] > 0.5
    current = states
    produced = states
    for step_index in range(STEPS):
        produced = lax.map(lambda operands: apply_section(*operands), (current, norm_gain, w_in, w_out, routes[:, step_index], route_weights[:, step_index]))
        if step_index + 1 < STEPS:
            current = jnp.where(live_mask, produced[source], jnp.zeros_like(produced))
    return produced
```

```python
import jax
import jax.numpy as jnp
from jax import lax
from jax.experimental import pallas as pl
from jax.experimental.pallas import tpu as pltpu
from jax.sharding import PartitionSpec as P

MESH = pl.DeviceIdType.MESH
BF16, F32 = jnp.bfloat16, jnp.float32

STEPS = 2
EPS = 1e-06
TOK = 64
D = 3584
NG = 4
GC = D // NG
HID = 512
RING = 8
BLK = 80

CHUNKS = ((1, 7), (2, 6), (3, 5), (4, 0))
SEND_ORDER = (1, 7, 2, 6, 3, 5, 4)
PLACE = {k: (j, b) for j, pair in enumerate(CHUNKS) for b, k in enumerate(pair)}


def iota(shape, dim):
    return lax.broadcasted_iota(jnp.int32, shape, dim)


def dot(a, b):
    return jnp.dot(a, b, preferred_element_type=F32)


def dot_rows(a, b):
    return lax.dot_general(a, b, (((0,), (0,)), ((), ())), preferred_element_type=F32)


def kernel(
    states, gain, w_in_hbm, w_out_hbm, routes, route_weights, out,
    w_in, w_out, x_in, x_out, normed, tx, rx, po, pr, zs, ret, lhs, hid, tail,
    z_send, z_recv, f_send, f_recv, p_send, p_recv, r_send, r_recv, s_send, s_recv, w_sem,
):
    pipe = lax.axis_index("pipe")
    expert = lax.axis_index("expert")
    dp = lax.axis_index("dp")
    z, half = expert // 2, expert % 2
    section = dp * 15 + (1 - 2 * dp) * pipe

    def holder(of_section):
        of_dp = of_section // 8
        return (of_dp * 15 + (1 - 2 * of_dp) * of_section, expert, of_dp)

    def on_ring(k):
        return (pipe, (z + k) % RING * 2 + half, dp)

    partner = (pipe, z * 2 + 1 - half, dp)
    after, before = holder((section + 1) % 16), holder((section + 15) % 16)

    barrier = pltpu.get_barrier_semaphore()
    peers = [on_ring(k) for k in range(1, RING)] + [partner, after, before]
    for peer in peers:
        pl.semaphore_signal(barrier, inc=1, device_id=peer, device_id_type=MESH)

    load_in = pltpu.make_async_copy(w_in_hbm.at[0, 0], w_in, w_sem.at[0])
    load_out = pltpu.make_async_copy(w_out_hbm.at[0, 0], w_out, w_sem.at[1])
    load_in.start()
    load_out.start()

    def send(src, dst, sems, index, peer):
        copy = pltpu.make_async_remote_copy(
            src_ref=src, dst_ref=dst, send_sem=sems[0].at[index], recv_sem=sems[1].at[index],
            device_id=peer, device_id_type=MESH,
        )
        copy.start()
        return copy

    ra, ca = iota((16, 64), 0), iota((16, 64), 1)
    same = (ra // 4 == ca // 16) & (ra % 4 == ca % 4)
    unstack = [jnp.where(same & (ca % 16 // 4 == g), 1.0, 0.0).astype(BF16) for g in range(NG)]
    rb, cb = iota((64, 64), 0), iota((64, 64), 1)
    restack = jnp.where(
        (rb // 16 == cb % 16 // 4) & (rb % 16 // 4 == cb // 16) & (rb % 4 == cb % 4), 1.0, 0.0
    ).astype(BF16)
    below = jnp.where(iota((TOK, TOK), 0) > iota((TOK, TOK), 1), 1.0, 0.0).astype(BF16)
    col = iota((TOK, 128), 1)
    expert_of = (z + col // 16) % RING

    def routing(step):
        first = routes[0, step, :, 0:1] == expert_of
        second = routes[0, step, :, 1:2] == expert_of
        named = jnp.where(first | second, 1.0, 0.0)
        weight = jnp.where(first, route_weights[0, step, :, 0:1], 0.0) + jnp.where(
            second, route_weights[0, step, :, 1:2], 0.0
        )
        slot = dot(below, named.astype(BF16)).astype(jnp.int32)
        in_main = slot == col % 16
        in_tail = slot == 16 + col % 4
        masks = [in_main] + [in_tail & (col % 16 // 4 == g) for g in range(NG)]
        pick = [jnp.where(m, named, 0.0).astype(BF16) for m in masks]
        mix = [jnp.where(m, weight, 0.0) for m in masks]
        high = [m.astype(BF16) for m in mix]
        low = [(m - h.astype(F32)).astype(BF16) for m, h in zip(mix, high)]

        def whole(parts):
            return [jnp.concatenate([parts[0], parts[1 + g]], axis=1) for g in range(NG)]

        return whole(pick), whole(high), whole(low)

    waits = []
    shift = []
    for step in range(STEPS):
        pick, high, low = routing(step)

        if step == 0:
            for g in range(NG):
                x_in[step, g] = states[0, :, g * GC : (g + 1) * GC]
        else:
            for copy in shift:
                copy.wait_recv()
            for g in range(NG):
                x_in[step, g] = jnp.where(section == 0, jnp.zeros((), BF16), x_in[step, g])
        squares = jnp.zeros((TOK, 1), F32)
        for g in range(NG):
            x = x_in[step, g].astype(F32)
            squares = squares + jnp.sum(x * x, axis=1, keepdims=True)
        scale = lax.rsqrt(squares / D + EPS)
        rest = jnp.zeros((128, GC), F32)
        for g in range(NG):
            x = x_in[step, g].astype(F32)
            normed = (x * scale * gain[0:1, g * GC : (g + 1) * GC]).astype(BF16)
            rows = dot_rows(pick[g], normed)
            tx[step, :, g * 16 : (g + 1) * 16, :] = rows[:128].astype(BF16).reshape(RING, 16, GC)
            rest = rest + rows[128:]
        tx[step, :, 64:80, :] = rest.astype(BF16).reshape(RING, 16, GC)

        if step == 0:
            pl.semaphore_wait(barrier, len(peers))

        j0, b0 = PLACE[0]
        forward = {}
        forward[0] = send(
            tx.at[step, 0], rx.at[step, j0, 2 + b0], (f_send.at[step], f_recv.at[step]), 0, partner
        )
        arrive = {}
        for k in SEND_ORDER:
            j, b = PLACE[k]
            arrive[k] = send(
                tx.at[step, k], rx.at[step, j, b], (z_send.at[step], z_recv.at[step]), k, on_ring(k)
            )
        rx[step, j0, b0] = tx[step, 0]

        def pass_on(j):
            for b, k in enumerate(CHUNKS[j]):
                if k:
                    arrive[k].wait_recv()
                    forward[k] = send(
                        rx.at[step, j, b], rx.at[step, j, 2 + b],
                        (f_send.at[step], f_recv.at[step]), k, partner,
                    )

        partial = {}

        def compute(j):
            for k in CHUNKS[j]:
                forward[k].wait_recv()
            for g in range(NG):
                columns = slice(g * GC, (g + 1) * GC)
                lhs[0:64, columns] = rx[step, j, :, g * 16 : (g + 1) * 16, :].reshape(64, GC)
                tails = rx[step, j, :, 64:80, :].reshape(64, GC)
                lhs[64:80, columns] = dot(unstack[g], tails).astype(BF16)

            if step == 0 and j == 0:
                load_in.wait()

            @pl.loop(0, 2)
            def _(n):
                at = pl.multiple_of(n * 256, 256)
                gate = dot(lhs[...], w_in[:, pl.ds(at, 256)])
                up = dot(lhs[...], w_in[:, pl.ds(pl.multiple_of(at + HID, 256), 256)])
                hid[:, pl.ds(at, 256)] = (gate / (1.0 + jnp.exp(-gate)) * up).astype(BF16)

            if step == 0 and j == 0:
                load_out.wait()

            @pl.loop(0, NG)
            def _(g):
                at = pl.multiple_of(g * GC, 128)
                y = dot(hid[...], w_out[:, pl.ds(at, GC)]).astype(BF16)
                row = pl.multiple_of(g * 16, 16)
                po[step, j, :, pl.ds(row, 16), :] = y[:64].reshape(4, 16, GC)
                tail[pl.ds(row, 16), :] = y[64:]

            po[step, j, :, 64:80, :] = dot(restack, tail[...]).astype(BF16).reshape(4, 16, GC)
            for b, k in enumerate(CHUNKS[j]):
                partial[k] = send(
                    po.at[step, j, 2 + b], pr.at[step, j, b],
                    (p_send.at[step], p_recv.at[step]), k, partner,
                )

        back = {}

        def give_back(j):
            for b, k in enumerate(CHUNKS[j]):
                partial[k].wait_recv()
                total = po[step, j, b].astype(F32) + pr[step, j, b].astype(F32)
                if k == 0:
                    ret[step, 0] = total.astype(BF16)
                else:
                    zs[step, j, b] = total.astype(BF16)
                    back[k] = send(
                        zs.at[step, j, b], ret.at[step, k],
                        (r_send.at[step], r_recv.at[step]), k, on_ring(RING - k),
                    )

        for tick in range(len(CHUNKS) + 2):
            if tick < len(CHUNKS):
                pass_on(tick)
            if 1 <= tick <= len(CHUNKS):
                compute(tick - 1)
            if tick >= 2:
                give_back(tick - 2)

        for k in back:
            back[k].wait_recv()
        for g in range(NG):
            main = ret[step, :, g * 16 : (g + 1) * 16, :].reshape(128, GC)
            tails = ret[step, :, 64:80, :].reshape(128, GC)
            rows = jnp.concatenate([main, tails], axis=0)
            total = dot(high[g], rows) + dot(low[g], rows)
            y = (x_in[step, g].astype(F32) + total).astype(BF16)
            if step + 1 < STEPS:
                x_out[g] = y
                shift.append(send(x_out.at[g], x_in.at[step + 1, g], (s_send, s_recv), g, after))
            else:
                out[0, :, g * GC : (g + 1) * GC] = y
        for copies in (arrive, forward, partial, back):
            waits.extend(copies.values())

    for copy in waits + shift:
        copy.wait_send()


def body(states, norm_gain, w_in, w_out, routes, route_weights):
    vmem, hbm = pl.BlockSpec(memory_space=pltpu.VMEM), pl.BlockSpec(memory_space=pl.ANY)
    sems = pltpu.SemaphoreType.DMA
    n = len(CHUNKS)
    return pl.pallas_call(
        kernel,
        out_shape=jax.ShapeDtypeStruct(states.shape, BF16),
        in_specs=[vmem, vmem, hbm, hbm, vmem, vmem],
        out_specs=vmem,
        scratch_shapes=[
            pltpu.VMEM((D, 2 * HID), BF16),
            pltpu.VMEM((HID, D), BF16),
            pltpu.VMEM((STEPS, NG, TOK, GC), BF16),
            pltpu.VMEM((NG, TOK, GC), BF16),
            pltpu.VMEM((NG, TOK, GC), BF16),
            pltpu.VMEM((STEPS, RING, BLK, GC), BF16),
            pltpu.VMEM((STEPS, n, 4, BLK, GC), BF16),
            pltpu.VMEM((STEPS, n, 4, BLK, GC), BF16),
            pltpu.VMEM((STEPS, n, 2, BLK, GC), BF16),
            pltpu.VMEM((STEPS, n, 2, BLK, GC), BF16),
            pltpu.VMEM((STEPS, RING, BLK, GC), BF16),
            pltpu.VMEM((BLK, D), BF16),
            pltpu.VMEM((BLK, HID), BF16),
            pltpu.VMEM((64, GC), BF16),
        ]
        + [sems((STEPS, RING))] * 8
        + [sems((NG,))] * 2
        + [sems((2,))],
        compiler_params=pltpu.CompilerParams(
            collective_id=0, has_side_effects=True, vmem_limit_bytes=56 * 2**20
        ),
        cost_estimate=pl.CostEstimate(
            flops=2 * 2 * 320 * 5505024, bytes_accessed=12 * 2**20, transcendentals=0
        ),
        name="cascade",
    )(states, norm_gain, w_in, w_out, routes, route_weights)


def solution(mesh):
    in_specs = (
        P(("pipe", "dp"), "expert", None),
        P(("pipe", "dp"), None),
        P(("pipe", "dp"), "expert", None, None),
        P(("pipe", "dp"), "expert", None, None),
        P(("pipe", "dp"), None, "expert", None),
        P(("pipe", "dp"), None, "expert", None),
    )
    out_specs = P(("pipe", "dp"), "expert", None)
    return jax.shard_map(body, mesh=mesh, in_specs=in_specs, out_specs=out_specs, check_vma=False)
```

```python
import jax
import jax.numpy as jnp
from jax import lax
from jax.experimental import pallas as pl
from jax.experimental.pallas import tpu as pltpu
from jax.sharding import PartitionSpec as P

MESH = pl.DeviceIdType.MESH
BF16, F32 = jnp.bfloat16, jnp.float32

STEPS = 2
EPS = 1e-06
TOK = 64
D = 3584
NG = 4
GC = D // NG
HID = 512
RING = 8
BLK = 80

CHUNKS = ((1, 0), (4, 7), (2, 6), (5, 3))
SEND_ORDER = (7, 5, 3, 2, 6, 1, 4)
AHEAD = 3
PROGRAM = (
    ("F", 7), ("F", 3), ("F", 5), ("F", 2), ("F", 6), ("C", 3), ("F", 4), ("C", 2),
    ("G", 3), ("F", 1), ("C", 1), ("G", 2), ("C", 0), ("G", 1), ("G", 0),
)


def iota(shape, dim):
    return lax.broadcasted_iota(jnp.int32, shape, dim)


def dot(a, b):
    return jnp.dot(a, b, preferred_element_type=F32)


def dot_rows(a, b):
    return lax.dot_general(a, b, (((0,), (0,)), ((), ())), preferred_element_type=F32)


def kernel(
    states, gain, w_in_hbm, w_out_hbm, routes, route_weights, out,
    w_in, w_out, x_in, x_out, pick, high, low, tx, rx, po, pr, zs, ret, lhs, hid, tail,
    z_send, z_recv, f_send, f_recv, p_send, p_recv, r_send, r_recv, s_send, s_recv, w_sem,
):
    pipe = lax.axis_index("pipe")
    expert = lax.axis_index("expert")
    dp = lax.axis_index("dp")
    z, half = expert // 2, expert % 2
    first_chunk = [which for act, which in PROGRAM if act == "C"][0]
    PLACE = {k: (j, b) for j, pair in enumerate(CHUNKS) for b, k in enumerate(pair)}
    section = dp * 15 + (1 - 2 * dp) * pipe

    def holder(of_section):
        of_dp = of_section // 8
        return (of_dp * 15 + (1 - 2 * of_dp) * of_section, expert, of_dp)

    def on_ring(k):
        return (pipe, (z + k) % RING * 2 + half, dp)

    partner = (pipe, z * 2 + 1 - half, dp)
    after, before = holder((section + 1) % 16), holder((section + 15) % 16)

    barrier = pltpu.get_barrier_semaphore()
    peers = [on_ring(k) for k in range(1, RING)] + [partner, after, before]
    for peer in peers:
        pl.semaphore_signal(barrier, inc=1, device_id=peer, device_id_type=MESH)

    load_in = pltpu.make_async_copy(w_in_hbm.at[0, 0], w_in, w_sem.at[0])
    load_out = pltpu.make_async_copy(w_out_hbm.at[0, 0], w_out, w_sem.at[1])
    load_in.start()
    load_out.start()

    def send(src, dst, sems, index, peer):
        copy = pltpu.make_async_remote_copy(
            src_ref=src, dst_ref=dst, send_sem=sems[0].at[index], recv_sem=sems[1].at[index],
            device_id=peer, device_id_type=MESH,
        )
        copy.start()
        return copy

    ra, ca = iota((16, 64), 0), iota((16, 64), 1)
    same = (ra // 4 == ca // 16) & (ra % 4 == ca % 4)
    unstack = [jnp.where(same & (ca % 16 // 4 == g), 1.0, 0.0).astype(BF16) for g in range(NG)]
    rb, cb = iota((64, 64), 0), iota((64, 64), 1)
    restack = jnp.where(
        (rb // 16 == cb % 16 // 4) & (rb % 16 // 4 == cb // 16) & (rb % 4 == cb % 4), 1.0, 0.0
    ).astype(BF16)
    below = jnp.where(iota((TOK, TOK), 0) > iota((TOK, TOK), 1), 1.0, 0.0).astype(BF16)
    col = iota((TOK, 128), 1)
    expert_of = (z + col // 16) % RING

    def routing(step, stage):
        ids = jnp.transpose(routes[0, step].astype(F32)).astype(jnp.int32)
        first, second = ids[:, 0:1] == expert_of, ids[:, 1:2] == expert_of
        named = jnp.where(first | second, 1.0, 0.0)
        slot = dot(below, named.astype(BF16)).astype(jnp.int32)
        in_main, in_tail = slot == col % 16, slot == 16 + col % 4
        if stage == "pick":
            value = named
        else:
            weights = jnp.transpose(route_weights[0, step])
            value = jnp.where(first, weights[:, 0:1], 0.0) + jnp.where(second, weights[:, 1:2], 0.0)
        for part in range(1 + NG):
            mask = in_main if part == 0 else in_tail & (col % 16 // 4 == part - 1)
            entry = jnp.where(mask, value, 0.0)
            near = entry.astype(BF16)
            rest = (entry - near.astype(F32)).astype(BF16)
            for g in range(NG) if part == 0 else (part - 1,):
                half = slice(0, 128) if part == 0 else slice(128, 256)
                if stage == "pick":
                    pick[step, g, :, half] = near
                else:
                    high[step, g, :, half] = near
                    low[step, g, :, half] = rest

    def hand_on(g):
        return pltpu.make_async_remote_copy(
            src_ref=x_out.at[g], dst_ref=x_in.at[1, g], send_sem=s_send.at[g], recv_sem=s_recv.at[g],
            device_id=after, device_id_type=MESH,
        )

    waits = []
    for step in range(STEPS):
        if step == 0:
            routing(step, "pick")

        if step == 0:
            for g in range(NG):
                x_in[step, g] = states[0, :, g * GC : (g + 1) * GC]
        else:
            @pl.when(section == 0)
            def _():
                x_in[step] = jnp.zeros((NG, TOK, GC), BF16)

            @pl.when(section > 0)
            def _():
                for g in range(NG):
                    hand_on(g).wait_recv()

        squares = jnp.zeros((TOK, 1), F32)
        for g in range(NG):
            x = x_in[step, g].astype(F32)
            squares = squares + jnp.sum(x * x, axis=1, keepdims=True)
        scale = lax.rsqrt(squares / D + EPS)
        rest = jnp.zeros((128, GC), F32)
        for g in range(NG):
            x = x_in[step, g].astype(F32)
            normed = (x * scale * gain[0:1, g * GC : (g + 1) * GC]).astype(BF16)
            rows = dot_rows(pick[step, g], normed)
            tx[step, :, g * 16 : (g + 1) * 16, :] = rows[:128].astype(BF16).reshape(RING, 16, GC)
            rest = rest + rows[128:]
        tx[step, :, 64:80, :] = rest.astype(BF16).reshape(RING, 16, GC)

        if step == 0:
            pl.semaphore_wait(barrier, len(peers))

        j0, b0 = PLACE[0]
        forward = {}
        forward[0] = send(
            tx.at[step, 0], rx.at[step, j0, 2 + b0], (f_send.at[step], f_recv.at[step]), 0, partner
        )
        arrive = {}

        def dispatch(k):
            j, b = PLACE[k]
            arrive[k] = send(
                tx.at[step, k], rx.at[step, j, b], (z_send.at[step], z_recv.at[step]), k, on_ring(k)
            )

        todo = list(SEND_ORDER)
        for _ in range(AHEAD):
            dispatch(todo.pop(0))
        rx[step, j0, b0] = tx[step, 0]
        if step == 0:
            for later in range(STEPS):
                if later:
                    routing(later, "pick")
                routing(later, "mix")

        def pass_on(k):
            arrive[k].wait_recv()
            if todo:
                dispatch(todo.pop(0))
            j, b = PLACE[k]
            forward[k] = send(
                rx.at[step, j, b], rx.at[step, j, 2 + b], (f_send.at[step], f_recv.at[step]), k, partner
            )

        partial = {}

        def compute(j):
            for k in CHUNKS[j]:
                forward[k].wait_recv()
            for g in range(NG):
                columns = slice(g * GC, (g + 1) * GC)
                lhs[0:64, columns] = rx[step, j, :, g * 16 : (g + 1) * 16, :].reshape(64, GC)
                tails = rx[step, j, :, 64:80, :].reshape(64, GC)
                lhs[64:80, columns] = dot(unstack[g], tails).astype(BF16)

            if step == 0 and j == first_chunk:
                load_in.wait()

            @pl.loop(0, 2)
            def _(n):
                at = pl.multiple_of(n * 256, 256)
                gate = dot(lhs[...], w_in[:, pl.ds(at, 256)])
                up = dot(lhs[...], w_in[:, pl.ds(pl.multiple_of(at + HID, 256), 256)])
                hid[:, pl.ds(at, 256)] = (gate / (1.0 + jnp.exp(-gate)) * up).astype(BF16)

            if step == 0 and j == first_chunk:
                load_out.wait()

            @pl.loop(0, NG)
            def _(g):
                at = pl.multiple_of(g * GC, 128)
                y = dot(hid[...], w_out[:, pl.ds(at, GC)]).astype(BF16)
                row = pl.multiple_of(g * 16, 16)
                po[step, j, :, pl.ds(row, 16), :] = y[:64].reshape(4, 16, GC)
                tail[pl.ds(row, 16), :] = y[64:]

            po[step, j, :, 64:80, :] = dot(restack, tail[...]).astype(BF16).reshape(4, 16, GC)
            for b, k in enumerate(CHUNKS[j]):
                partial[k] = send(
                    po.at[step, j, 2 + b], pr.at[step, j, b],
                    (p_send.at[step], p_recv.at[step]), k, partner,
                )

        back = {}

        def give_back(j):
            for b, k in enumerate(CHUNKS[j]):
                partial[k].wait_recv()
                total = po[step, j, b].astype(F32) + pr[step, j, b].astype(F32)
                if k == 0:
                    ret[step, 0] = total.astype(BF16)
                else:
                    zs[step, j, b] = total.astype(BF16)
                    back[k] = send(
                        zs.at[step, j, b], ret.at[step, k],
                        (r_send.at[step], r_recv.at[step]), k, on_ring(RING - k),
                    )

        for act, which in PROGRAM:
            {"F": pass_on, "C": compute, "G": give_back}[act](which)

        for k in back:
            back[k].wait_recv()
        for g in range(NG):
            main = ret[step, :, g * 16 : (g + 1) * 16, :].reshape(128, GC)
            tails = ret[step, :, 64:80, :].reshape(128, GC)
            rows = jnp.concatenate([main, tails], axis=0)
            total = dot(high[step, g], rows) + dot(low[step, g], rows)
            y = (x_in[step, g].astype(F32) + total).astype(BF16)
            if step + 1 < STEPS:
                x_out[g] = y

                @pl.when(section < 15)
                def _():
                    hand_on(g).start()

            else:
                out[0, :, g * GC : (g + 1) * GC] = y
        for copies in (arrive, forward, partial, back):
            waits.extend(copies.values())

    for copy in waits:
        copy.wait_send()

    @pl.when(section < 15)
    def _():
        for g in range(NG):
            hand_on(g).wait_send()


def body(states, norm_gain, w_in, w_out, routes, route_weights):
    vmem, hbm = pl.BlockSpec(memory_space=pltpu.VMEM), pl.BlockSpec(memory_space=pl.ANY)
    sems = pltpu.SemaphoreType.DMA
    n = len(CHUNKS)
    return pl.pallas_call(
        kernel,
        out_shape=jax.ShapeDtypeStruct(states.shape, BF16),
        in_specs=[vmem, vmem, hbm, hbm, vmem, vmem],
        out_specs=vmem,
        scratch_shapes=[
            pltpu.VMEM((D, 2 * HID), BF16),
            pltpu.VMEM((HID, D), BF16),
            pltpu.VMEM((STEPS, NG, TOK, GC), BF16),
            pltpu.VMEM((NG, TOK, GC), BF16),
            pltpu.VMEM((STEPS, NG, TOK, 256), BF16),
            pltpu.VMEM((STEPS, NG, TOK, 256), BF16),
            pltpu.VMEM((STEPS, NG, TOK, 256), BF16),
            pltpu.VMEM((STEPS, RING, BLK, GC), BF16),
            pltpu.VMEM((STEPS, n, 4, BLK, GC), BF16),
            pltpu.VMEM((STEPS, n, 4, BLK, GC), BF16),
            pltpu.VMEM((STEPS, n, 2, BLK, GC), BF16),
            pltpu.VMEM((STEPS, n, 2, BLK, GC), BF16),
            pltpu.VMEM((STEPS, RING, BLK, GC), BF16),
            pltpu.VMEM((BLK, D), BF16),
            pltpu.VMEM((BLK, HID), BF16),
            pltpu.VMEM((64, GC), BF16),
        ]
        + [sems((STEPS, RING))] * 8
        + [sems((NG,))] * 2
        + [sems((2,))],
        compiler_params=pltpu.CompilerParams(
            collective_id=0, has_side_effects=True, vmem_limit_bytes=56 * 2**20
        ),
        cost_estimate=pl.CostEstimate(
            flops=2 * 2 * 320 * 5505024, bytes_accessed=12 * 2**20, transcendentals=0
        ),
        name="cascade",
    )(states, norm_gain, w_in, w_out, jnp.swapaxes(routes, 2, 3), jnp.swapaxes(route_weights, 2, 3))


def solution(mesh):
    in_specs = (
        P(("pipe", "dp"), "expert", None),
        P(("pipe", "dp"), None),
        P(("pipe", "dp"), "expert", None, None),
        P(("pipe", "dp"), "expert", None, None),
        P(("pipe", "dp"), None, "expert", None),
        P(("pipe", "dp"), None, "expert", None),
    )
    out_specs = P(("pipe", "dp"), "expert", None)
    return jax.shard_map(body, mesh=mesh, in_specs=in_specs, out_specs=out_specs, check_vma=False)
```

```python
import jax
import jax.numpy as jnp
from jax import lax
from jax.experimental import pallas as pl
from jax.experimental.pallas import tpu as pltpu
from jax.sharding import PartitionSpec as P

MESH = pl.DeviceIdType.MESH
BF16, F32 = jnp.bfloat16, jnp.float32

STEPS = 2
EPS = 1e-06
TOK = 64
D = 3584
NG = 4
GC = D // NG
HID = 512
RING = 8
BLK = 80

CHUNKS = ((1, 0), (4, 7), (2, 6), (5, 3))
SEND_ORDER = (7, 5, 3, 2, 6, 1, 4)
AHEAD = 3
PROGRAM = (
    ("F", 7), ("F", 3), ("F", 5), ("F", 2), ("F", 6), ("C", 3), ("F", 4), ("C", 2),
    ("G", 3), ("F", 1), ("C", 1), ("G", 2), ("C", 0), ("G", 1), ("G", 0),
)


def iota(shape, dim):
    return lax.broadcasted_iota(jnp.int32, shape, dim)


def dot(a, b):
    return jnp.dot(a, b, preferred_element_type=F32)


def dot_rows(a, b):
    return lax.dot_general(a, b, (((0,), (0,)), ((), ())), preferred_element_type=F32)


def kernel(
    states, gain, w_in_hbm, w_out_hbm, routes, route_weights, out,
    w_in, w_out, x_in, x_out, pick, high, low, tx, rx, po, pr, zs, ret, lhs, hid, tail,
    z_send, z_recv, f_send, f_recv, p_send, p_recv, r_send, r_recv, s_send, s_recv, w_sem, x_sem,
):
    pipe = lax.axis_index("pipe")
    expert = lax.axis_index("expert")
    dp = lax.axis_index("dp")
    z, half = expert // 2, expert % 2
    first_chunk = [which for act, which in PROGRAM if act == "C"][0]
    PLACE = {k: (j, b) for j, pair in enumerate(CHUNKS) for b, k in enumerate(pair)}
    section = dp * 15 + (1 - 2 * dp) * pipe

    def holder(of_section):
        of_dp = of_section // 8
        return (of_dp * 15 + (1 - 2 * of_dp) * of_section, expert, of_dp)

    def on_ring(k):
        return (pipe, (z + k) % RING * 2 + half, dp)

    partner = (pipe, z * 2 + 1 - half, dp)
    after, before = holder((section + 1) % 16), holder((section + 15) % 16)

    loads = [
        pltpu.make_async_copy(states.at[0, :, pl.ds(g * GC, GC)], x_in.at[0, g], x_sem.at[g])
        for g in range(NG)
    ]
    for load in loads:
        load.start()

    barrier = pltpu.get_barrier_semaphore()
    peers = [on_ring(k) for k in range(1, RING)] + [partner, after, before]
    for peer in peers:
        pl.semaphore_signal(barrier, inc=1, device_id=peer, device_id_type=MESH)

    load_in = pltpu.make_async_copy(w_in_hbm.at[0, 0], w_in, w_sem.at[0])
    load_out = pltpu.make_async_copy(w_out_hbm.at[0, 0], w_out, w_sem.at[1])
    load_in.start()
    load_out.start()

    def send(src, dst, sems, index, peer):
        copy = pltpu.make_async_remote_copy(
            src_ref=src, dst_ref=dst, send_sem=sems[0].at[index], recv_sem=sems[1].at[index],
            device_id=peer, device_id_type=MESH,
        )
        copy.start()
        return copy

    ra, ca = iota((16, 64), 0), iota((16, 64), 1)
    same = (ra // 4 == ca // 16) & (ra % 4 == ca % 4)
    unstack = [jnp.where(same & (ca % 16 // 4 == g), 1.0, 0.0).astype(BF16) for g in range(NG)]
    rb, cb = iota((64, 64), 0), iota((64, 64), 1)
    restack = jnp.where(
        (rb // 16 == cb % 16 // 4) & (rb % 16 // 4 == cb // 16) & (rb % 4 == cb % 4), 1.0, 0.0
    ).astype(BF16)
    below = jnp.where(iota((TOK, TOK), 0) > iota((TOK, TOK), 1), 1.0, 0.0).astype(BF16)
    col = iota((TOK, 128), 1)
    expert_of = (z + col // 16) % RING

    def routing(step, stage):
        ids = jnp.transpose(routes[0, step].astype(F32)).astype(jnp.int32)
        first, second = ids[:, 0:1] == expert_of, ids[:, 1:2] == expert_of
        named = jnp.where(first | second, 1.0, 0.0)
        slot = dot(below, named.astype(BF16)).astype(jnp.int32)
        in_main, in_tail = slot == col % 16, slot == 16 + col % 4
        if stage == "pick":
            value = named
        else:
            weights = jnp.transpose(route_weights[0, step])
            value = jnp.where(first, weights[:, 0:1], 0.0) + jnp.where(second, weights[:, 1:2], 0.0)
        for part in range(1 + NG):
            mask = in_main if part == 0 else in_tail & (col % 16 // 4 == part - 1)
            entry = jnp.where(mask, value, 0.0)
            near = entry.astype(BF16)
            rest = (entry - near.astype(F32)).astype(BF16)
            for g in range(NG) if part == 0 else (part - 1,):
                half = slice(0, 128) if part == 0 else slice(128, 256)
                if stage == "pick":
                    pick[step, g, :, half] = near
                else:
                    high[step, g, :, half] = near
                    low[step, g, :, half] = rest

    def hand_on(g):
        return pltpu.make_async_remote_copy(
            src_ref=x_out.at[g], dst_ref=x_in.at[1, g], send_sem=s_send.at[g], recv_sem=s_recv.at[g],
            device_id=after, device_id_type=MESH,
        )

    waits = []
    for step in range(STEPS):
        if step == 0:
            routing(step, "pick")

        if step == 0:
            for load in loads:
                load.wait()
        else:
            @pl.when(section == 0)
            def _():
                x_in[step] = jnp.zeros((NG, TOK, GC), BF16)

            @pl.when(section > 0)
            def _():
                for g in range(NG):
                    hand_on(g).wait_recv()

        squares = jnp.zeros((TOK, 1), F32)
        for g in range(NG):
            x = x_in[step, g].astype(F32)
            squares = squares + jnp.sum(x * x, axis=1, keepdims=True)
        scale = lax.rsqrt(squares / D + EPS)
        rest = jnp.zeros((128, GC), F32)
        for g in range(NG):
            x = x_in[step, g].astype(F32)
            normed = (x * scale * gain[0:1, g * GC : (g + 1) * GC]).astype(BF16)
            rows = dot_rows(pick[step, g], normed)
            tx[step, :, g * 16 : (g + 1) * 16, :] = rows[:128].astype(BF16).reshape(RING, 16, GC)
            rest = rest + rows[128:]
        tx[step, :, 64:80, :] = rest.astype(BF16).reshape(RING, 16, GC)

        if step == 0:
            pl.semaphore_wait(barrier, len(peers))

        j0, b0 = PLACE[0]
        forward = {}
        forward[0] = send(
            tx.at[step, 0], rx.at[step, j0, 2 + b0], (f_send.at[step], f_recv.at[step]), 0, partner
        )
        arrive = {}

        def dispatch(k):
            j, b = PLACE[k]
            arrive[k] = send(
                tx.at[step, k], rx.at[step, j, b], (z_send.at[step], z_recv.at[step]), k, on_ring(k)
            )

        todo = list(SEND_ORDER)
        for _ in range(AHEAD):
            dispatch(todo.pop(0))
        rx[step, j0, b0] = tx[step, 0]
        if step == 0:
            for later in range(STEPS):
                if later:
                    routing(later, "pick")
                routing(later, "mix")

        def pass_on(k):
            arrive[k].wait_recv()
            if todo:
                dispatch(todo.pop(0))
            j, b = PLACE[k]
            forward[k] = send(
                rx.at[step, j, b], rx.at[step, j, 2 + b], (f_send.at[step], f_recv.at[step]), k, partner
            )

        partial = {}

        def compute(j):
            for k in CHUNKS[j]:
                forward[k].wait_recv()
            for g in range(NG):
                columns = slice(g * GC, (g + 1) * GC)
                lhs[0:64, columns] = rx[step, j, :, g * 16 : (g + 1) * 16, :].reshape(64, GC)
                tails = rx[step, j, :, 64:80, :].reshape(64, GC)
                lhs[64:80, columns] = dot(unstack[g], tails).astype(BF16)

            if step == 0 and j == first_chunk:
                load_in.wait()

            @pl.loop(0, 2)
            def _(n):
                at = pl.multiple_of(n * 256, 256)
                gate = dot(lhs[...], w_in[:, pl.ds(at, 256)])
                up = dot(lhs[...], w_in[:, pl.ds(pl.multiple_of(at + HID, 256), 256)])
                hid[:, pl.ds(at, 256)] = (gate / (1.0 + jnp.exp(-gate)) * up).astype(BF16)

            if step == 0 and j == first_chunk:
                load_out.wait()

            @pl.loop(0, NG)
            def _(g):
                at = pl.multiple_of(g * GC, 128)
                y = dot(hid[...], w_out[:, pl.ds(at, GC)]).astype(BF16)
                row = pl.multiple_of(g * 16, 16)
                po[step, j, :, pl.ds(row, 16), :] = y[:64].reshape(4, 16, GC)
                tail[pl.ds(row, 16), :] = y[64:]

            po[step, j, :, 64:80, :] = dot(restack, tail[...]).astype(BF16).reshape(4, 16, GC)
            for b, k in enumerate(CHUNKS[j]):
                partial[k] = send(
                    po.at[step, j, 2 + b], pr.at[step, j, b],
                    (p_send.at[step], p_recv.at[step]), k, partner,
                )

        back = {}

        def give_back(j):
            for b, k in enumerate(CHUNKS[j]):
                partial[k].wait_recv()
                total = po[step, j, b].astype(F32) + pr[step, j, b].astype(F32)
                if k == 0:
                    ret[step, 0] = total.astype(BF16)
                else:
                    zs[step, j, b] = total.astype(BF16)
                    back[k] = send(
                        zs.at[step, j, b], ret.at[step, k],
                        (r_send.at[step], r_recv.at[step]), k, on_ring(RING - k),
                    )

        for act, which in PROGRAM:
            {"F": pass_on, "C": compute, "G": give_back}[act](which)

        for k in back:
            back[k].wait_recv()
        for g in range(NG):
            main = ret[step, :, g * 16 : (g + 1) * 16, :].reshape(128, GC)
            tails = ret[step, :, 64:80, :].reshape(128, GC)
            rows = jnp.concatenate([main, tails], axis=0)
            total = dot(high[step, g], rows) + dot(low[step, g], rows)
            y = (x_in[step, g].astype(F32) + total).astype(BF16)
            if step + 1 < STEPS:
                x_out[g] = y

                @pl.when(section < 15)
                def _():
                    hand_on(g).start()

            else:
                out[0, :, g * GC : (g + 1) * GC] = y
        for copies in (arrive, forward, partial, back):
            waits.extend(copies.values())

    for copy in waits:
        copy.wait_send()

    @pl.when(section < 15)
    def _():
        for g in range(NG):
            hand_on(g).wait_send()


def body(states, norm_gain, w_in, w_out, routes, route_weights):
    vmem, hbm = pl.BlockSpec(memory_space=pltpu.VMEM), pl.BlockSpec(memory_space=pl.ANY)
    sems = pltpu.SemaphoreType.DMA
    n = len(CHUNKS)
    return pl.pallas_call(
        kernel,
        out_shape=jax.ShapeDtypeStruct(states.shape, BF16),
        in_specs=[hbm, vmem, hbm, hbm, vmem, vmem],
        out_specs=vmem,
        scratch_shapes=[
            pltpu.VMEM((D, 2 * HID), BF16),
            pltpu.VMEM((HID, D), BF16),
            pltpu.VMEM((STEPS, NG, TOK, GC), BF16),
            pltpu.VMEM((NG, TOK, GC), BF16),
            pltpu.VMEM((STEPS, NG, TOK, 256), BF16),
            pltpu.VMEM((STEPS, NG, TOK, 256), BF16),
            pltpu.VMEM((STEPS, NG, TOK, 256), BF16),
            pltpu.VMEM((STEPS, RING, BLK, GC), BF16),
            pltpu.VMEM((STEPS, n, 4, BLK, GC), BF16),
            pltpu.VMEM((STEPS, n, 4, BLK, GC), BF16),
            pltpu.VMEM((STEPS, n, 2, BLK, GC), BF16),
            pltpu.VMEM((STEPS, n, 2, BLK, GC), BF16),
            pltpu.VMEM((STEPS, RING, BLK, GC), BF16),
            pltpu.VMEM((BLK, D), BF16),
            pltpu.VMEM((BLK, HID), BF16),
            pltpu.VMEM((64, GC), BF16),
        ]
        + [sems((STEPS, RING))] * 8
        + [sems((NG,))] * 2
        + [sems((2,)), sems((NG,))],
        compiler_params=pltpu.CompilerParams(
            collective_id=0, has_side_effects=True, vmem_limit_bytes=56 * 2**20
        ),
        cost_estimate=pl.CostEstimate(
            flops=2 * 2 * 320 * 5505024, bytes_accessed=12 * 2**20, transcendentals=0
        ),
        name="cascade",
    )(states, norm_gain, w_in, w_out, jnp.swapaxes(routes, 2, 3), jnp.swapaxes(route_weights, 2, 3))


def solution(mesh):
    in_specs = (
        P(("pipe", "dp"), "expert", None),
        P(("pipe", "dp"), None),
        P(("pipe", "dp"), "expert", None, None),
        P(("pipe", "dp"), "expert", None, None),
        P(("pipe", "dp"), None, "expert", None),
        P(("pipe", "dp"), None, "expert", None),
    )
    out_specs = P(("pipe", "dp"), "expert", None)
    return jax.shard_map(body, mesh=mesh, in_specs=in_specs, out_specs=out_specs, check_vma=False)
```
